32 devices in a mesh: rep: 8 (over y, x, core), fsdp: 4 (over z).
Axes of the slice: x: 2, y: 2, z: 4, core: 2. Of those that a mesh axis runs over, the one named last changes fastest.
Arguments:
- tokens: bfloat16 [32768, 8192], P(('rep', 'fsdp')), may hold values from -6 to 6
- norm_gain: bfloat16 [8192], replicated, may hold values from 0.25 to 1.75
- deltas: bfloat16 [8, 8192, 1024], P('rep', 'fsdp'), may hold values from -0.09375 to 0.09375
- inner_steps: int32 [8, 16], replicated, may hold values from 1 to 64
- bucket_of_row: int32 [8192], P('fsdp'), may hold values from 0 to 15, never falling along the last dimension, each value on 1 to 1024 neighbouring positions
- master: float32 [8192, 1024], P(('fsdp', 'rep')), may hold values from -0.0625 to 0.0625
- momentum: float32 [8192, 1024], P(('fsdp', 'rep')), may hold values from -0.0625 to 0.0625
Outputs:
- keys: bfloat16 [32768, 1024], P(('rep', 'fsdp'))
- master_new: float32 [8192, 1024], P(('fsdp', 'rep'))
- momentum_new: float32 [8192, 1024], P(('fsdp', 'rep'))
The draws below stay inside these ranges and needn't reach their ends.
Inputs may be any that keep to these rules, and one draw needn't show every extreme that they name: `bucket_of_row`: never falls along the rows; each bucket holds 1 to 1024 rows.
All inputs are finite; a program needn't handle non-finite values.
Results may differ from the reference program's by a relative error of at most 0.0058.
Values may be sent and summed in bfloat16 or wider, within the bound.
No kernel may reach another device: no remote copies, remote signals or barrier semaphores. Data moves between devices by JAX's collectives and lax.ppermute only.
A program may use at most 192 MiB of HBM per device.

```python
import math
import jax
import jax.numpy as jnp
import numpy as np
from jax import lax

D = 8192
KV = 1024
TOK_DEV = 1024
NB = 16
REPS = 8
TOKENS = 32768
BUCKET_MOST = 1024


def touch_ends(values, own_key, low, top_value):
    place = [jax.random.randint(jax.random.fold_in(own_key, axis), (), 0, length) for axis, length in enumerate(values.shape)]
    widest = values.shape.index(max(values.shape))
    neighbour = place[:widest] + [(place[widest] + 1) % values.shape[widest]] + place[widest + 1:]
    return values.at[tuple(place)].set(low).at[tuple(neighbour)].set(top_value)


def raised(drawn, own_key, source, target, parts, factor):
    owner, partner = [(jnp.arange(drawn.shape[axis_at]) // (drawn.shape[axis_at] // parts)).reshape([-1 if axis == axis_at else 1 for axis in range(drawn.ndim)]) for axis_at in (source, target)]
    chosen = jax.random.permutation(own_key, parts)[partner]
    strong = (owner == chosen) | (owner == (partner + parts // 2) % parts)
    return jnp.where(strong, factor * drawn, drawn)


def level_of(rng, shape, pieces, smallest, largest):
    loudness = 1.0
    for dim, blocks in pieces:
        steps = jax.random.uniform(jax.random.fold_in(jax.random.fold_in(rng, 6), dim), (blocks,), jnp.float32, smallest / len(pieces), largest / len(pieces))
        loudness = loudness * jnp.repeat(jnp.exp(steps), shape[dim] // blocks).reshape((-1,) + (1,) * (len(shape) - 1 - dim))
    return loudness


def length_profile(amount, total, most, slope):
    loads = [(1 << 20) // math.isqrt(standing ** slope) + 1 for standing in range(2, amount + 1)]
    surplus, holding = total - most - (amount - 1), [1] * (amount - 1)
    while surplus > 0:
        movable = [i for i in range(amount - 1) if holding[i] < most]
        mass, budget = sum([loads[i] for i in movable]), surplus
        for i in movable:
            more = min(most - holding[i], max(1, budget * loads[i] // mass), surplus)
            holding[i] = holding[i] + more
            surplus = surplus - more
    return np.array([most] + holding)


def uneven_parts(rng, amount, total, limit, slope):
    if amount == 2:
        one = jax.random.randint(rng, (), max(1, total - limit), min(limit, total - 1) + 1)
        return jnp.stack([one, total - one])
    lengths = jnp.asarray(length_profile(amount, total, limit, slope), jnp.int32)
    twos = (amount - 1) // 2
    source_of, taker = lengths[1:1 + 2 * twos:2], lengths[2:2 + 2 * twos:2]
    slack = jnp.minimum(source_of - 1, limit - taker)
    shifted = jax.random.randint(jax.random.fold_in(rng, 1), (twos,), 0, 1 << 20) % (slack + 1)
    lengths = lengths.at[1:1 + 2 * twos:2].set(source_of - shifted).at[2:2 + 2 * twos:2].set(taker + shifted)
    return lengths[jax.random.permutation(jax.random.fold_in(rng, 2), amount)]


def normal_values(own_key, shape, spread, most, split=(), kind=jnp.bfloat16):
    result = spread * jax.random.normal(own_key, shape, jnp.float32)
    if split:
        result = result * level_of(own_key, shape, split, -0.22, 0.18)
    return jnp.clip(result, -most, most).astype(kind)


def noise_with(rng, extent, width, bound, split, heavy, dtype=jnp.bfloat16):
    entries = width * jax.random.normal(rng, extent, jnp.float32)
    if split:
        entries = entries * level_of(rng, extent, split, -0.22, 0.18)
    return jnp.clip(raised(entries, jax.random.fold_in(rng, 3), *heavy), -bound, bound).astype(dtype)


def setup_inputs(seed: int = 0) -> dict:
    splits = jax.random.split(jax.random.key(seed), 8)
    return {
        "tokens": normal_values(splits[0], (TOKENS, D), 1.0, 6.0, ((0, 32),)),
        "norm_gain": jnp.clip(1.0 + 0.15 * jax.random.normal(splits[1], (D,), jnp.float32), 0.25, 1.75).astype(jnp.bfloat16),
        "deltas": noise_with(splits[2], (REPS, D, KV), D ** -0.5, 0.09375, ((0, 8), (1, 4)), (0, 1, 8, 2.0)),
        "inner_steps": touch_ends(jax.random.randint(splits[3], (REPS, NB), 1, 65), jax.random.fold_in(splits[3], 1), 1, 64).astype(jnp.int32),
        "bucket_of_row": jnp.searchsorted(jnp.cumsum(uneven_parts(splits[4], NB, D, BUCKET_MOST, 1)), jnp.arange(D), side="right").astype(jnp.int32),
        "master": normal_values(splits[5], (D, KV), D ** -0.5, 0.0625, ((0, 32),), jnp.float32),
        "momentum": normal_values(splits[6], (D, KV), D ** -0.5, 0.0625, ((0, 32),), jnp.float32),
    }


OUTER_RATE = 0.7
MOMENTUM_KEEP = 0.9
EPSILON = 1e-05

def normalize(rows, norm_gain):
    values = rows.astype(jnp.float32)
    scale = lax.rsqrt(lax.optimization_barrier(jnp.mean(values * values, axis=1, keepdims=True)) + EPSILON)
    return (values * scale * norm_gain.astype(jnp.float32)[None, :]).astype(jnp.bfloat16)

def reference(tokens, norm_gain, deltas, inner_steps, bucket_of_row, master, momentum):
    counts = inner_steps.astype(jnp.float32)
    share = counts / lax.optimization_barrier(jnp.sum(counts, axis=0, keepdims=True))
    row_weight = share[:, bucket_of_row]

    def add_one(total, pair):
        weight_row, delta = pair
        return (total + weight_row[:, None] * delta.astype(jnp.float32), None)
    averaged, _ = lax.scan(add_one, jnp.zeros(master.shape, jnp.float32), (row_weight, deltas))
    momentum_new = MOMENTUM_KEEP * momentum + averaged
    master_new = master - OUTER_RATE * (averaged + MOMENTUM_KEEP * momentum_new)
    layer = master_new.astype(jnp.bfloat16)
    blocks = tokens.reshape(-1, TOK_DEV, tokens.shape[1])

    def project(rows):
        normed = normalize(rows, norm_gain)
        return jnp.dot(normed, layer, preferred_element_type=jnp.float32).astype(jnp.bfloat16)
    keys = lax.map(project, blocks).reshape(tokens.shape[0], layer.shape[1])
    return (keys, master_new, momentum_new)
```

```python
import functools

import jax
import jax.numpy as jnp
from jax import lax
from jax.experimental import pallas as pl
from jax.experimental.pallas import tpu as pltpu
from jax.sharding import PartitionSpec as P

OUTER_RATE = 0.7
MOMENTUM_KEEP = 0.9
EPSILON = 1e-05
VMEM_BYTES = 48 * 1024 * 1024

CORE, ALONG_X, ALONG_Y = 1, 2, 4


def flip(value, even_bit, odd_bit):
    perm = [(i, i ^ (odd_bit if i & CORE else even_bit)) for i in range(8)]
    return lax.ppermute(value, "rep", perm)


def swap_cores(value):
    return flip(value, CORE, CORE)


def swap_first(value):
    return flip(value, ALONG_X, ALONG_Y)


def swap_second(value):
    return flip(value, ALONG_Y, ALONG_X)


def row_weights(inner_steps, bucket_of_row, replica):
    counts = inner_steps.astype(jnp.float32)
    share = counts / jnp.sum(counts, axis=0, keepdims=True)
    own = lax.dynamic_index_in_dim(share, replica, 0, keepdims=False)
    bucket_ids = jnp.arange(counts.shape[1], dtype=jnp.int32)
    one_hot = (bucket_of_row[:, None] == bucket_ids[None, :]).astype(jnp.float32)
    return jnp.sum(one_hot * own[None, :], axis=1)


def outer_step(averaged, master, momentum):
    momentum_new = MOMENTUM_KEEP * momentum + averaged
    master_new = master - OUTER_RATE * (averaged + MOMENTUM_KEEP * momentum_new)
    return master_new, momentum_new


def normalize_kernel(order, tokens, gain, *outs, width):
    values = tokens[...].astype(jnp.float32)
    scale = lax.rsqrt(jnp.mean(values * values, axis=1, keepdims=True) + EPSILON)
    per_out = outs[0].shape[1] // width
    for at, out in enumerate(outs):
        for j in range(per_out):
            source = pl.ds(pl.multiple_of(order[at * per_out + j] * width, width), width)
            part = tokens[:, source].astype(jnp.float32) * scale * gain[:, source].astype(jnp.float32)
            out[:, j * width:(j + 1) * width] = part.astype(out.dtype)


def normalize_in_order(tokens, gain, order, width, parts):
    rows, features = tokens.shape
    tile = 128
    return pl.pallas_call(
        functools.partial(normalize_kernel, width=width),
        grid_spec=pltpu.PrefetchScalarGridSpec(
            num_scalar_prefetch=1,
            grid=(rows // tile,),
            in_specs=[
                pl.BlockSpec((tile, features), lambda i, order: (i, 0)),
                pl.BlockSpec((1, features), lambda i, order: (0, 0)),
            ],
            out_specs=[pl.BlockSpec((tile, features // parts), lambda i, order: (i, 0))] * parts,
        ),
        out_shape=[jax.ShapeDtypeStruct((rows, features // parts), tokens.dtype)] * parts,
        compiler_params=pltpu.CompilerParams(vmem_limit_bytes=VMEM_BYTES),
        cost_estimate=pl.CostEstimate(
            flops=rows * features * 6, bytes_accessed=rows * features * 4, transcendentals=rows
        ),
        name="normalize_in_order",
    )(order, tokens, gain.reshape(1, features))


def project_kernel(first, last, normed, *refs):
    total = None
    pieces = refs[: len(refs) - (1 if first else 2)]
    start = 0
    for piece in pieces:
        depth = piece.shape[0]
        term = jnp.dot(
            normed[:, start:start + depth], piece[...], preferred_element_type=jnp.float32
        )
        total = term if total is None else total + term
        start += depth
    if not first:
        total = total + refs[-2][...]
    refs[-1][...] = total.astype(refs[-1].dtype)


def project(normed, pieces, total, last):
    rows, depth = normed.shape
    cols = pieces[0].shape[1]
    tile = 256
    first = total is None
    row_spec = pl.BlockSpec((tile, cols), lambda i: (i, 0))
    return pl.pallas_call(
        functools.partial(project_kernel, first, last),
        grid=(rows // tile,),
        in_specs=[pl.BlockSpec((tile, depth), lambda i: (i, 0))]
        + [pl.BlockSpec(piece.shape, lambda i: (0, 0)) for piece in pieces]
        + ([] if first else [row_spec]),
        out_specs=row_spec,
        out_shape=jax.ShapeDtypeStruct((rows, cols), normed.dtype if last else jnp.float32),
        compiler_params=pltpu.CompilerParams(vmem_limit_bytes=VMEM_BYTES),
        cost_estimate=pl.CostEstimate(
            flops=2 * rows * depth * cols,
            bytes_accessed=2 * (rows * depth + depth * cols) + 8 * rows * cols,
            transcendentals=0,
        ),
        name="project",
    )(normed, *pieces, *([] if first else [total]))


def gather_along_line(own):
    place = lax.axis_index("fsdp")
    outer = (place == 0) | (place == 3)
    pair = lax.ppermute(own, "fsdp", [(0, 1), (1, 0), (2, 3), (3, 2)])
    inner_near = lax.ppermute(own, "fsdp", [(1, 2), (2, 1)])
    inner_far = lax.ppermute(pair, "fsdp", [(1, 2), (2, 1)])
    outer_near = lax.ppermute(inner_near, "fsdp", [(1, 0), (2, 3)])
    outer_far = lax.ppermute(inner_far, "fsdp", [(1, 0), (2, 3)])
    near = jnp.where(outer, outer_near, inner_near)
    far = jnp.where(outer, outer_far, inner_far)
    return [own, pair, near, far]


def on_block(tokens, norm_gain, deltas, inner_steps, bucket_of_row, master, momentum):
    rep, place = lax.axis_index("rep"), lax.axis_index("fsdp")
    core = rep & 1
    sibling = rep ^ CORE
    first_bit = jnp.where(core == 0, ALONG_X, ALONG_Y)
    second_bit = jnp.where(core == 0, ALONG_Y, ALONG_X)
    rows, cols = master.shape
    order8 = jnp.stack([
        rep, rep ^ first_bit, rep ^ second_bit, rep ^ 6,
        sibling, sibling ^ second_bit, sibling ^ first_bit, sibling ^ 6,
    ])
    low = place < 2
    order4 = jnp.stack([place, place ^ 1, jnp.where(low, 2, 1), jnp.where(low, 3, 0)])
    order = (order4[:, None] * 8 + order8[None, :]).reshape(-1).astype(jnp.int32)

    own_delta = deltas[0].reshape(4, 2, rows, cols)
    received = swap_cores(lax.dynamic_index_in_dim(own_delta, 1 - core, 1, keepdims=False))
    kept = lax.dynamic_index_in_dim(own_delta, core, 1, keepdims=False)
    weights = [
        lax.dynamic_index_in_dim(
            row_weights(inner_steps, bucket_of_row, r).reshape(4, 2, rows), core, 1, keepdims=False
        )
        for r in (rep, sibling)
    ]

    def chip_sum(replica):
        at = replica // 2

        def pick(array):
            return lax.dynamic_index_in_dim(array, at, 0, keepdims=False)

        return (
            pick(weights[0])[:, None] * pick(kept).astype(jnp.float32)
            + pick(weights[1])[:, None] * pick(received).astype(jnp.float32)
        )

    link = deltas.dtype
    away = rep ^ first_bit
    to_first = jnp.concatenate([chip_sum(away), chip_sum(away ^ second_bit)], 0).astype(link)
    from_first = swap_first(to_first)
    to_second = chip_sum(rep ^ second_bit) + from_first[rows:].astype(jnp.float32)
    from_second = swap_second(to_second.astype(link))
    averaged = chip_sum(rep) + from_first[:rows].astype(jnp.float32) + from_second.astype(jnp.float32)
    master_new, momentum_new = outer_step(averaged, master, momentum)
    layer = master_new.astype(link)

    normed = normalize_in_order(tokens, norm_gain, order, rows, 4)
    total = None
    for at, block in enumerate(gather_along_line(layer)):
        half = jnp.concatenate([block, swap_first(block)], 0)
        other = swap_second(half)
        pieces = [half, other, swap_cores(half), swap_cores(other)]
        total = project(normed[at], pieces, total, at == 3)
    return total, master_new, momentum_new


def on_any(tokens, norm_gain, deltas, inner_steps, bucket_of_row, master, momentum):
    weight = row_weights(inner_steps, bucket_of_row, lax.axis_index("rep"))
    weighted = weight[:, None] * deltas[0].astype(jnp.float32)
    averaged = lax.psum_scatter(weighted, "rep", scatter_dimension=0, tiled=True)
    master_new, momentum_new = outer_step(averaged, master, momentum)
    layer = lax.all_gather(master_new.astype(deltas.dtype), ("fsdp", "rep"), axis=0, tiled=True)
    features = tokens.shape[1]
    order = jnp.arange(features // 256, dtype=jnp.int32)
    (normed,) = normalize_in_order(tokens, norm_gain, order, 256, 1)
    keys = jnp.dot(normed, layer, preferred_element_type=jnp.float32).astype(tokens.dtype)
    return keys, master_new, momentum_new


def solution(mesh):
    in_specs = (
        P(("rep", "fsdp"), None),
        P(),
        P("rep", "fsdp", None),
        P(),
        P("fsdp"),
        P(("fsdp", "rep"), None),
        P(("fsdp", "rep"), None),
    )
    out_specs = (P(("rep", "fsdp"), None), P(("fsdp", "rep"), None), P(("fsdp", "rep"), None))
    is_block = mesh.shape["rep"] == 8 and mesh.shape["fsdp"] == 4
    return jax.shard_map(
        on_block if is_block else on_any,
        mesh=mesh, in_specs=in_specs, out_specs=out_specs, check_vma=False,
    )
```

```python
import functools

import jax
import jax.numpy as jnp
from jax import lax
from jax.experimental import pallas as pl
from jax.experimental.pallas import tpu as pltpu
from jax.sharding import PartitionSpec as P

OUTER_RATE = 0.7
MOMENTUM_KEEP = 0.9
EPSILON = 1e-05
VMEM_BYTES = 24 * 1024 * 1024

CORE, ALONG_X, ALONG_Y = 1, 2, 4


def flip(value, even_bit, odd_bit):
    perm = [(i, i ^ (odd_bit if i & CORE else even_bit)) for i in range(8)]
    return lax.ppermute(value, "rep", perm)


def swap_cores(value):
    return flip(value, CORE, CORE)


def swap_first(value):
    return flip(value, ALONG_X, ALONG_Y)


def swap_second(value):
    return flip(value, ALONG_Y, ALONG_X)


def row_weights(inner_steps, bucket_of_row, replica):
    counts = inner_steps.astype(jnp.float32)
    share = counts / jnp.sum(counts, axis=0, keepdims=True)
    own = lax.dynamic_index_in_dim(share, replica, 0, keepdims=False)
    bucket_ids = jnp.arange(counts.shape[1], dtype=jnp.int32)
    one_hot = (bucket_of_row[:, None] == bucket_ids[None, :]).astype(jnp.float32)
    return jnp.sum(one_hot * own[None, :], axis=1)


def outer_step(averaged, master, momentum):
    momentum_new = MOMENTUM_KEEP * momentum + averaged
    master_new = master - OUTER_RATE * (averaged + MOMENTUM_KEEP * momentum_new)
    return master_new, momentum_new


def normalize_kernel(order, tokens, gain, *refs, width, parts):
    outs = refs[len(refs) - parts - 1:-1]
    refs[-1][...] = jnp.zeros_like(refs[-1])
    values = tokens[...].astype(jnp.float32)
    scale = lax.rsqrt(jnp.mean(values * values, axis=1, keepdims=True) + EPSILON)
    at = 0
    for out in outs:
        for j in range(out.shape[1] // width):
            source = pl.ds(pl.multiple_of(order[at] * width, width), width)
            at += 1
            part = tokens[:, source].astype(jnp.float32) * scale * gain[:, source].astype(jnp.float32)
            out[:, j * width:(j + 1) * width] = part.astype(out.dtype)


def normalize_in_order(tokens, gain, order, width, parts, first=0, count=None, earlier=()):
    rows, features = tokens.shape
    tile = 128
    count = rows // tile if count is None else count
    return list(pl.pallas_call(
        functools.partial(normalize_kernel, width=width, parts=len(parts)),
        grid_spec=pltpu.PrefetchScalarGridSpec(
            num_scalar_prefetch=1,
            grid=(count,),
            in_specs=[
                pl.BlockSpec((tile, features), lambda i, order: (i + first, 0)),
                pl.BlockSpec((1, features), lambda i, order: (0, 0)),
            ] + [pl.BlockSpec(memory_space=pl.ANY)] * len(earlier),
            out_specs=[pl.BlockSpec((tile, part), lambda i, order: (i + first, 0)) for part in parts]
            + [pl.BlockSpec((8, 128), lambda i, order: (0, 0))],
        ),
        out_shape=[pltpu.HBM((rows, part), tokens.dtype) for part in parts]
        + [jax.ShapeDtypeStruct((8, 128), jnp.float32)],
        input_output_aliases={3 + i: i for i in range(len(earlier))},
        compiler_params=pltpu.CompilerParams(vmem_limit_bytes=VMEM_BYTES),
        cost_estimate=pl.CostEstimate(
            flops=count * tile * features * 6,
            bytes_accessed=count * tile * features * 4,
            transcendentals=count * tile,
        ),
        name="normalize_in_order",
    )(order, tokens, gain.reshape(1, features), *earlier))


def project_kernel(depths, normed, *refs):
    total = None
    start = 0
    for depth, piece in zip(depths, refs):
        term = jnp.dot(
            normed[:, start:start + depth], piece[...], preferred_element_type=jnp.float32
        )
        total = term if total is None else total + term
        start += depth
    if refs[-2].shape == total.shape:
        total = total + refs[-2][...]
    refs[-1][...] = total.astype(refs[-1].dtype)


def project(normed, pieces, total, last=False):
    rows = normed.shape[0]
    cols = pieces[0].shape[1]
    depths = [piece.shape[0] for piece in pieces]
    depth = sum(depths)
    tile = 256
    first = total.shape != (rows, cols)
    row_spec = pl.BlockSpec((tile, cols), lambda i: (i, 0))
    return pl.pallas_call(
        functools.partial(project_kernel, depths),
        grid=(rows // tile,),
        in_specs=[pl.BlockSpec((tile, depth), lambda i: (i, 0))]
        + [pl.BlockSpec(memory_space=pltpu.VMEM) for piece in pieces]
        + [pl.BlockSpec(memory_space=pl.ANY) if first else row_spec],
        out_specs=row_spec,
        out_shape=jax.ShapeDtypeStruct((rows, cols), normed.dtype if last else jnp.float32),
        compiler_params=pltpu.CompilerParams(vmem_limit_bytes=VMEM_BYTES),
        cost_estimate=pl.CostEstimate(
            flops=2 * rows * depth * cols,
            bytes_accessed=2 * (rows * depth + depth * cols) + 8 * rows * cols,
            transcendentals=0,
        ),
        name="project",
    )(normed, *pieces, total)


def together(*values):
    return lax.optimization_barrier(values)


def to_pair(value):
    return lax.ppermute(value, "fsdp", [(0, 1), (1, 0), (2, 3), (3, 2)])


def inwards(value):
    return lax.ppermute(value, "fsdp", [(1, 2), (2, 1)])


def outwards(value):
    return lax.ppermute(value, "fsdp", [(1, 0), (2, 3)])


def on_block(tokens, norm_gain, deltas, inner_steps, bucket_of_row, master, momentum):
    rep, place = lax.axis_index("rep"), lax.axis_index("fsdp")
    core = rep & 1
    sibling = rep ^ CORE
    first_bit = jnp.where(core == 0, ALONG_X, ALONG_Y)
    second_bit = jnp.where(core == 0, ALONG_Y, ALONG_X)
    rows, cols = master.shape
    tokens = pltpu.with_memory_space_constraint(tokens, pltpu.HBM)
    order8 = jnp.stack([
        rep, rep ^ first_bit, sibling, sibling ^ second_bit,
        rep ^ second_bit, rep ^ 6, sibling ^ first_bit, sibling ^ 6,
    ])
    low = place < 2
    order4 = jnp.stack([place, place ^ 1, jnp.where(low, 2, 1), jnp.where(low, 3, 0)])
    order = (order4[:, None] * 8 + order8[None, :]).reshape(-1).astype(jnp.int32)
    parts = [4 * rows, 8 * rows, 8 * rows, 8 * rows, 4 * rows]

    link = deltas.dtype
    half_rows = rows // 2
    own_delta = deltas[0].reshape(4, 2, 2, half_rows, cols)
    weights = [
        row_weights(inner_steps, bucket_of_row, r).reshape(4, 2, 2, half_rows) for r in (rep, sibling)
    ]

    def pick(array, *index):
        starts = index + (0,) * (array.ndim - len(index))
        sizes = (1,) * len(index) + array.shape[len(index):]
        return lax.dynamic_slice(array, starts, sizes).reshape(array.shape[len(index):])

    def chip_sum(replica, part, received):
        at = replica // 2
        return (
            pick(weights[0], at, core, part)[:, None]
            * pick(own_delta, at, core, part).astype(jnp.float32)
            + pick(weights[1], at, core, part)[:, None] * pick(received, at).astype(jnp.float32)
        )

    received = []
    for part in range(2):
        theirs = lax.dynamic_slice(own_delta, (0, 1 - core, part, 0, 0), (4, 1, 1, half_rows, cols))
        received.append(swap_cores(theirs.reshape(4, half_rows, cols)))
    away = rep ^ first_bit
    from_first = []
    for part in range(2):
        to_first = jnp.concatenate(
            [chip_sum(block, part, received[part]) for block in (away, away ^ second_bit)], 0
        ).astype(link)
        from_first.append(swap_first(to_first))
        received, order, to_first = together(received, order, to_first)
    normed = normalize_in_order(tokens, norm_gain, order, rows, parts, 0, 4)
    own_sum = [chip_sum(rep, part, received[part]) for part in range(2)]
    next_sum = [chip_sum(rep ^ second_bit, part, received[part]) for part in range(2)]
    from_first[0], own_sum, next_sum, normed[-1] = together(from_first[0], own_sum, next_sum, normed[-1])
    from_second = []
    for part in range(2):
        next_sum[part] += from_first[part][half_rows:].astype(jnp.float32)
        own_sum[part] += from_first[part][:half_rows].astype(jnp.float32)
        to_second = next_sum[part].astype(link)
        from_second.append(swap_second(to_second))
        order, to_second = together(order, to_second)
    normed = normalize_in_order(tokens, norm_gain, order, rows, parts, 4, 4, normed)
    from_second[0], normed[-1] = together(from_second[0], normed[-1])
    from_second, own_sum = together(from_second, own_sum)
    averaged = jnp.concatenate(
        [own_sum[part] + from_second[part].astype(jnp.float32) for part in range(2)], 0
    )
    master_new, momentum_new = outer_step(averaged, master, momentum)
    layer = master_new.astype(link)

    outer = (place == 0) | (place == 3)
    pair, near_in = to_pair(layer), inwards(layer)
    beside = swap_first(layer)
    half = jnp.concatenate([layer, beside], 0)
    other = swap_second(half)
    pieces = [half, swap_cores(half)]
    far_in, near_out = inwards(pair), outwards(near_in)
    beside = swap_first(pair)

    beside, other, far_in, near_out = together(beside, other, far_in, near_out)
    half = jnp.concatenate([pair, beside], 0)
    far_out = outwards(far_in)
    near = jnp.where(outer, near_out, near_in)
    last = [other, swap_cores(other)]
    other = swap_second(half)
    beside = swap_first(near)
    half, pieces = together(half, pieces)
    total = project(normed[0], pieces, normed[-1])
    pieces = last + [half, swap_cores(half)]
    far = jnp.where(outer, far_out, far_in)

    beside, other, total = together(beside, other, total)
    half = jnp.concatenate([near, beside], 0)
    last = [other, swap_cores(other)]
    other = swap_second(half)
    beside = swap_first(far)
    half, pieces = together(half, pieces)
    total = project(normed[1], pieces, total)
    pieces = last + [half, swap_cores(half)]

    beside, other, total = together(beside, other, total)
    half = jnp.concatenate([far, beside], 0)
    last = [other, swap_cores(other)]
    other = swap_second(half)
    half, pieces = together(half, pieces)
    total = project(normed[2], pieces, total)
    pieces = last + [half, swap_cores(half)]
    other, total = together(other, total)
    total = project(normed[3], pieces, total)
    last = [other, swap_cores(other)]
    total = project(normed[4], last, total, True)
    return total, master_new, momentum_new


def on_any(tokens, norm_gain, deltas, inner_steps, bucket_of_row, master, momentum):
    weight = row_weights(inner_steps, bucket_of_row, lax.axis_index("rep"))
    weighted = weight[:, None] * deltas[0].astype(jnp.float32)
    averaged = lax.psum_scatter(weighted, "rep", scatter_dimension=0, tiled=True)
    master_new, momentum_new = outer_step(averaged, master, momentum)
    layer = lax.all_gather(master_new.astype(deltas.dtype), ("fsdp", "rep"), axis=0, tiled=True)
    features = tokens.shape[1]
    order = jnp.arange(features // 256, dtype=jnp.int32)
    normed, _ = normalize_in_order(tokens, norm_gain, order, 256, [features])
    keys = jnp.dot(normed, layer, preferred_element_type=jnp.float32).astype(tokens.dtype)
    return keys, master_new, momentum_new


def solution(mesh):
    in_specs = (
        P(("rep", "fsdp"), None),
        P(),
        P("rep", "fsdp", None),
        P(),
        P("fsdp"),
        P(("fsdp", "rep"), None),
        P(("fsdp", "rep"), None),
    )
    out_specs = (P(("rep", "fsdp"), None), P(("fsdp", "rep"), None), P(("fsdp", "rep"), None))
    is_block = mesh.shape["rep"] == 8 and mesh.shape["fsdp"] == 4
    return jax.shard_map(
        on_block if is_block else on_any,
        mesh=mesh, in_specs=in_specs, out_specs=out_specs, check_vma=False,
    )
```

```python
import functools

import jax
import jax.numpy as jnp
from jax import lax
from jax.experimental import pallas as pl
from jax.experimental.pallas import tpu as pltpu
from jax.sharding import PartitionSpec as P

OUTER_RATE = 0.7
MOMENTUM_KEEP = 0.9
EPSILON = 1e-05
VMEM_BYTES = 24 * 1024 * 1024

CORE, ALONG_X, ALONG_Y = 1, 2, 4


def flip(value, even_bit, odd_bit):
    perm = [(i, i ^ (odd_bit if i & CORE else even_bit)) for i in range(8)]
    return lax.ppermute(value, "rep", perm)


def swap_cores(value):
    return flip(value, CORE, CORE)


def swap_first(value):
    return flip(value, ALONG_X, ALONG_Y)


def swap_second(value):
    return flip(value, ALONG_Y, ALONG_X)


def row_weights(inner_steps, bucket_of_row, replica):
    counts = inner_steps.astype(jnp.float32)
    share = counts / jnp.sum(counts, axis=0, keepdims=True)
    own = lax.dynamic_index_in_dim(share, replica, 0, keepdims=False)
    bucket_ids = jnp.arange(counts.shape[1], dtype=jnp.int32)
    one_hot = (bucket_of_row[:, None] == bucket_ids[None, :]).astype(jnp.float32)
    return jnp.sum(one_hot * own[None, :], axis=1)


def outer_step(averaged, master, momentum):
    momentum_new = MOMENTUM_KEEP * momentum + averaged
    master_new = master - OUTER_RATE * (averaged + MOMENTUM_KEEP * momentum_new)
    return master_new, momentum_new


def normalize_kernel(order, tokens, gain, *refs, width, parts):
    outs = refs[len(refs) - parts - 1:-1]
    refs[-1][...] = jnp.zeros_like(refs[-1])
    values = tokens[...].astype(jnp.float32)
    scale = lax.rsqrt(jnp.mean(values * values, axis=1, keepdims=True) + EPSILON)
    at = 0
    for out in outs:
        for j in range(out.shape[1] // width):
            source = pl.ds(pl.multiple_of(order[at] * width, width), width)
            at += 1
            part = tokens[:, source].astype(jnp.float32) * scale * gain[:, source].astype(jnp.float32)
            out[:, j * width:(j + 1) * width] = part.astype(out.dtype)


def normalize_in_order(tokens, gain, order, width, parts, first=0, count=None, earlier=()):
    rows, features = tokens.shape
    tile = 128
    count = rows // tile if count is None else count
    return list(pl.pallas_call(
        functools.partial(normalize_kernel, width=width, parts=len(parts)),
        grid_spec=pltpu.PrefetchScalarGridSpec(
            num_scalar_prefetch=1,
            grid=(count,),
            in_specs=[
                pl.BlockSpec((tile, features), lambda i, order: (i + first, 0)),
                pl.BlockSpec((1, features), lambda i, order: (0, 0)),
            ] + [pl.BlockSpec(memory_space=pl.ANY)] * len(earlier),
            out_specs=[pl.BlockSpec((tile, part), lambda i, order: (i + first, 0)) for part in parts]
            + [pl.BlockSpec((8, 128), lambda i, order: (0, 0))],
        ),
        out_shape=[pltpu.HBM((rows, part), tokens.dtype) for part in parts]
        + [jax.ShapeDtypeStruct((8, 128), jnp.float32)],
        input_output_aliases={3 + i: i for i in range(len(earlier))},
        compiler_params=pltpu.CompilerParams(vmem_limit_bytes=VMEM_BYTES),
        cost_estimate=pl.CostEstimate(
            flops=count * tile * features * 6,
            bytes_accessed=count * tile * features * 4,
            transcendentals=count * tile,
        ),
        name="normalize_in_order",
    )(order, tokens, gain.reshape(1, features), *earlier))


def project_kernel(depths, normed, *refs):
    total = None
    start = 0
    for depth, piece in zip(depths, refs):
        term = jnp.dot(
            normed[:, start:start + depth], piece[...], preferred_element_type=jnp.float32
        )
        total = term if total is None else total + term
        start += depth
    if refs[-2].shape == total.shape:
        total = total + refs[-2][...]
    refs[-1][...] = total.astype(refs[-1].dtype)


def project(normed, pieces, total, last=False):
    rows = normed.shape[0]
    cols = pieces[0].shape[1]
    depths = [piece.shape[0] for piece in pieces]
    depth = sum(depths)
    tile = 256
    first = total.shape != (rows, cols)
    row_spec = pl.BlockSpec((tile, cols), lambda i: (i, 0))
    return pl.pallas_call(
        functools.partial(project_kernel, depths),
        grid=(rows // tile,),
        in_specs=[pl.BlockSpec((tile, depth), lambda i: (i, 0))]
        + [pl.BlockSpec(memory_space=pltpu.VMEM) for piece in pieces]
        + [pl.BlockSpec(memory_space=pl.ANY) if first else row_spec],
        out_specs=row_spec,
        out_shape=jax.ShapeDtypeStruct((rows, cols), normed.dtype if last else jnp.float32),
        compiler_params=pltpu.CompilerParams(vmem_limit_bytes=VMEM_BYTES),
        cost_estimate=pl.CostEstimate(
            flops=2 * rows * depth * cols,
            bytes_accessed=2 * (rows * depth + depth * cols) + 8 * rows * cols,
            transcendentals=0,
        ),
        name="project",
    )(normed, *pieces, total)


def together(*values):
    return lax.optimization_barrier(values)


def to_pair(value):
    return lax.ppermute(value, "fsdp", [(0, 1), (1, 0), (2, 3), (3, 2)])


def inwards(value):
    return lax.ppermute(value, "fsdp", [(1, 2), (2, 1)])


def outwards(value):
    return lax.ppermute(value, "fsdp", [(1, 0), (2, 3)])


def on_block(tokens, norm_gain, deltas, inner_steps, bucket_of_row, master, momentum):
    rep, place = lax.axis_index("rep"), lax.axis_index("fsdp")
    core = rep & 1
    sibling = rep ^ CORE
    first_bit = jnp.where(core == 0, ALONG_X, ALONG_Y)
    second_bit = jnp.where(core == 0, ALONG_Y, ALONG_X)
    rows, cols = master.shape
    tokens = pltpu.with_memory_space_constraint(tokens, pltpu.HBM)
    low = place < 2
    block_place = [place, place ^ 1, jnp.where(low, 2, 1), jnp.where(low, 3, 0)]
    half_reps = [rep, rep ^ first_bit, sibling, sibling ^ second_bit]
    other_reps = [rep ^ second_bit, rep ^ 6, sibling ^ first_bit, sibling ^ 6]
    sequence = [
        [(0, half_reps)],
        [(0, other_reps), (1, half_reps)],
        [(2, half_reps), (2, other_reps)],
        [(3, half_reps)],
        [(1, other_reps), (3, other_reps)],
    ]
    order = jnp.stack([
        block_place[at] * 8 + r for group in sequence for at, reps in group for r in reps
    ]).astype(jnp.int32)
    parts = [4 * rows * len(group) for group in sequence]

    link = deltas.dtype
    half_rows = rows // 2
    own_delta = deltas[0].reshape(4, 2, 2, half_rows, cols)
    weights = [
        row_weights(inner_steps, bucket_of_row, r).reshape(4, 2, 2, half_rows) for r in (rep, sibling)
    ]

    def pick(array, *index):
        starts = index + (0,) * (array.ndim - len(index))
        sizes = (1,) * len(index) + array.shape[len(index):]
        return lax.dynamic_slice(array, starts, sizes).reshape(array.shape[len(index):])

    def chip_sum(replica, part, received):
        at = replica // 2
        return (
            pick(weights[0], at, core, part)[:, None]
            * pick(own_delta, at, core, part).astype(jnp.float32)
            + pick(weights[1], at, core, part)[:, None] * pick(received, at).astype(jnp.float32)
        )

    received = []
    not_mine = 1 - core
    for part in range(2):
        theirs = lax.dynamic_slice(own_delta, (0, not_mine, part, 0, 0), (4, 1, 1, half_rows, cols))
        theirs = theirs.reshape(4, half_rows, cols)
        received.append(swap_cores(theirs))
        not_mine, theirs = together(not_mine, theirs)
    away = rep ^ first_bit
    from_first = []
    for part in range(2):
        to_first = jnp.concatenate(
            [chip_sum(block, part, received[part]) for block in (away, away ^ second_bit)], 0
        ).astype(link)
        from_first.append(swap_first(to_first))
        received, order, to_first = together(received, order, to_first)
    normed = normalize_in_order(tokens, norm_gain, order, rows, parts, 0, 2)
    own_sum = [chip_sum(rep, part, received[part]) for part in range(2)]
    next_sum = [chip_sum(rep ^ second_bit, part, received[part]) for part in range(2)]
    from_first[0], own_sum, next_sum, normed[-1] = together(from_first[0], own_sum, next_sum, normed[-1])
    from_second = []
    for part in range(2):
        next_sum[part] += from_first[part][half_rows:].astype(jnp.float32)
        own_sum[part] += from_first[part][:half_rows].astype(jnp.float32)
        to_second = next_sum[part].astype(link)
        from_second.append(swap_second(to_second))
        order, to_second = together(order, to_second)
    normed = normalize_in_order(tokens, norm_gain, order, rows, parts, 2, 2, normed)
    from_second[0], normed[-1] = together(from_second[0], normed[-1])
    from_second, own_sum = together(from_second, own_sum)
    averaged = jnp.concatenate(
        [own_sum[part] + from_second[part].astype(jnp.float32) for part in range(2)], 0
    )
    master_new, momentum_new = outer_step(averaged, master, momentum)
    layer = master_new.astype(link)

    outer = (place == 0) | (place == 3)
    pair, near_in = to_pair(layer), inwards(layer)
    pair, near_in = together(pair, near_in)
    beside = swap_first(layer)
    half0 = jnp.concatenate([layer, beside], 0)
    other0 = swap_second(half0)
    half0 = [half0, swap_cores(half0)]
    far_in, near_out = inwards(pair), outwards(near_in)
    beside = swap_first(pair)

    order, pair = together(order, pair)
    normed = normalize_in_order(tokens, norm_gain, order, rows, parts, 4, 4, normed)
    beside, other0, near_out, normed[-1] = together(beside, other0, near_out, normed[-1])
    near = jnp.where(outer, near_out, near_in)
    half1 = jnp.concatenate([pair, beside], 0)
    beside = swap_first(near)
    far_out = outwards(far_in)
    half1, half0 = together(half1, half0)
    total = project(normed[0], half0, normed[-1])
    ready = [other0, swap_cores(other0), half1, swap_cores(half1)]

    beside, total = together(beside, total)
    half2 = jnp.concatenate([near, beside], 0)
    other2 = swap_second(half2)
    far = jnp.where(outer, far_out, far_in)
    far, pair_source = together(far, other0)
    beside = swap_first(far)
    other1 = to_pair(pair_source)
    half2, ready = together(half2, ready)
    total = project(normed[1], ready, total)

    beside, other2, total = together(beside, other2, total)
    half3 = jnp.concatenate([far, beside], 0)
    other3 = swap_second(half3)
    ready = [half2, swap_cores(half2), other2, swap_cores(other2)]
    half3, ready = together(half3, ready)
    total = project(normed[2], ready, total)
    half3 = [half3, swap_cores(half3)]
    other3, total = together(other3, total)
    total = project(normed[3], half3, total)
    last = [other1, swap_cores(other1), other3, swap_cores(other3)]
    total = project(normed[4], last, total, True)
    return total, master_new, momentum_new


def on_any(tokens, norm_gain, deltas, inner_steps, bucket_of_row, master, momentum):
    weight = row_weights(inner_steps, bucket_of_row, lax.axis_index("rep"))
    weighted = weight[:, None] * deltas[0].astype(jnp.float32)
    averaged = lax.psum_scatter(weighted, "rep", scatter_dimension=0, tiled=True)
    master_new, momentum_new = outer_step(averaged, master, momentum)
    layer = lax.all_gather(master_new.astype(deltas.dtype), ("fsdp", "rep"), axis=0, tiled=True)
    features = tokens.shape[1]
    order = jnp.arange(features // 256, dtype=jnp.int32)
    normed, _ = normalize_in_order(tokens, norm_gain, order, 256, [features])
    keys = jnp.dot(normed, layer, preferred_element_type=jnp.float32).astype(tokens.dtype)
    return keys, master_new, momentum_new


def solution(mesh):
    in_specs = (
        P(("rep", "fsdp"), None),
        P(),
        P("rep", "fsdp", None),
        P(),
        P("fsdp"),
        P(("fsdp", "rep"), None),
        P(("fsdp", "rep"), None),
    )
    out_specs = (P(("rep", "fsdp"), None), P(("fsdp", "rep"), None), P(("fsdp", "rep"), None))
    is_block = mesh.shape["rep"] == 8 and mesh.shape["fsdp"] == 4
    return jax.shard_map(
        on_block if is_block else on_any,
        mesh=mesh, in_specs=in_specs, out_specs=out_specs, check_vma=False,
    )
```

```python
import functools

import jax
import jax.numpy as jnp
from jax import lax
from jax.experimental import pallas as pl
from jax.experimental.pallas import tpu as pltpu
from jax.sharding import PartitionSpec as P

OUTER_RATE = 0.7
MOMENTUM_KEEP = 0.9
EPSILON = 1e-05
VMEM_BYTES = 24 * 1024 * 1024

CORE, ALONG_X, ALONG_Y = 1, 2, 4


def flip(value, even_bit, odd_bit):
    perm = [(i, i ^ (odd_bit if i & CORE else even_bit)) for i in range(8)]
    return lax.ppermute(value, "rep", perm)


def swap_cores(value):
    return flip(value, CORE, CORE)


def swap_first(value):
    return flip(value, ALONG_X, ALONG_Y)


def swap_second(value):
    return flip(value, ALONG_Y, ALONG_X)


def row_weights(inner_steps, bucket_of_row, replica):
    counts = inner_steps.astype(jnp.float32)
    share = counts / jnp.sum(counts, axis=0, keepdims=True)
    own = lax.dynamic_index_in_dim(share, replica, 0, keepdims=False)
    bucket_ids = jnp.arange(counts.shape[1], dtype=jnp.int32)
    one_hot = (bucket_of_row[:, None] == bucket_ids[None, :]).astype(jnp.float32)
    return jnp.sum(one_hot * own[None, :], axis=1)


def outer_step(averaged, master, momentum):
    momentum_new = MOMENTUM_KEEP * momentum + averaged
    master_new = master - OUTER_RATE * (averaged + MOMENTUM_KEEP * momentum_new)
    return master_new, momentum_new


def normalize_kernel(order, tokens, gain, *refs, width, parts):
    outs = refs[len(refs) - parts - 1:-1]
    refs[-1][...] = jnp.zeros_like(refs[-1])
    values = tokens[...].astype(jnp.float32)
    scale = lax.rsqrt(jnp.mean(values * values, axis=1, keepdims=True) + EPSILON)
    at = 0
    for out in outs:
        for j in range(out.shape[1] // width):
            source = pl.ds(pl.multiple_of(order[at] * width, width), width)
            at += 1
            part = tokens[:, source].astype(jnp.float32) * scale * gain[:, source].astype(jnp.float32)
            out[:, j * width:(j + 1) * width] = part.astype(out.dtype)


def normalize_in_order(tokens, gain, order, width, parts, first=0, count=None, earlier=()):
    rows, features = tokens.shape
    tile = 128
    count = rows // tile if count is None else count
    return list(pl.pallas_call(
        functools.partial(normalize_kernel, width=width, parts=len(parts)),
        grid_spec=pltpu.PrefetchScalarGridSpec(
            num_scalar_prefetch=1,
            grid=(count,),
            in_specs=[
                pl.BlockSpec((tile, features), lambda i, order: (i + first, 0)),
                pl.BlockSpec((1, features), lambda i, order: (0, 0)),
            ] + [pl.BlockSpec(memory_space=pl.ANY)] * len(earlier),
            out_specs=[pl.BlockSpec((tile, part), lambda i, order: (i + first, 0)) for part in parts]
            + [pl.BlockSpec((8, 128), lambda i, order: (0, 0))],
        ),
        out_shape=[pltpu.HBM((rows, part), tokens.dtype) for part in parts]
        + [jax.ShapeDtypeStruct((8, 128), jnp.float32)],
        input_output_aliases={3 + i: i for i in range(len(earlier))},
        compiler_params=pltpu.CompilerParams(vmem_limit_bytes=VMEM_BYTES),
        cost_estimate=pl.CostEstimate(
            flops=count * tile * features * 6,
            bytes_accessed=count * tile * features * 4,
            transcendentals=count * tile,
        ),
        name="normalize_in_order",
    )(order, tokens, gain.reshape(1, features), *earlier))


def project_kernel(depths, normed, *refs):
    total = None
    start = 0
    for depth, piece in zip(depths, refs):
        term = jnp.dot(
            normed[:, start:start + depth], piece[...], preferred_element_type=jnp.float32
        )
        total = term if total is None else total + term
        start += depth
    if refs[-2].shape == total.shape:
        total = total + refs[-2][...]
    refs[-1][...] = total.astype(refs[-1].dtype)


def project(normed, pieces, total, last=False):
    rows = normed.shape[0]
    cols = pieces[0].shape[1]
    depths = [piece.shape[0] for piece in pieces]
    depth = sum(depths)
    tile = 256
    first = total.shape != (rows, cols)
    row_spec = pl.BlockSpec((tile, cols), lambda i: (i, 0))
    return pl.pallas_call(
        functools.partial(project_kernel, depths),
        grid=(rows // tile,),
        in_specs=[pl.BlockSpec((tile, depth), lambda i: (i, 0))]
        + [pl.BlockSpec(memory_space=pltpu.VMEM) for piece in pieces]
        + [pl.BlockSpec(memory_space=pl.ANY) if first else row_spec],
        out_specs=row_spec,
        out_shape=jax.ShapeDtypeStruct((rows, cols), normed.dtype if last else jnp.float32),
        compiler_params=pltpu.CompilerParams(vmem_limit_bytes=VMEM_BYTES),
        cost_estimate=pl.CostEstimate(
            flops=2 * rows * depth * cols,
            bytes_accessed=2 * (rows * depth + depth * cols) + 8 * rows * cols,
            transcendentals=0,
        ),
        name="project",
    )(normed, *pieces, total)


def together(*values):
    return lax.optimization_barrier(values)


def to_pair(value):
    return lax.ppermute(value, "fsdp", [(0, 1), (1, 0), (2, 3), (3, 2)])


def inwards(value):
    return lax.ppermute(value, "fsdp", [(1, 2), (2, 1)])


def outwards(value):
    return lax.ppermute(value, "fsdp", [(1, 0), (2, 3)])


def on_block(tokens, norm_gain, deltas, inner_steps, bucket_of_row, master, momentum):
    rep, place = lax.axis_index("rep"), lax.axis_index("fsdp")
    core = rep & 1
    sibling = rep ^ CORE
    first_bit = jnp.where(core == 0, ALONG_X, ALONG_Y)
    second_bit = jnp.where(core == 0, ALONG_Y, ALONG_X)
    rows, cols = master.shape
    tokens = pltpu.with_memory_space_constraint(tokens, pltpu.HBM)
    low = place < 2
    block_place = [place, place ^ 1, jnp.where(low, 2, 1), jnp.where(low, 3, 0)]
    half_reps = [rep, rep ^ first_bit, sibling, sibling ^ second_bit]
    other_reps = [rep ^ second_bit, rep ^ 6, sibling ^ first_bit, sibling ^ 6]
    sequence = [
        [(0, half_reps)],
        [(0, other_reps), (1, half_reps), (1, other_reps[0::2])],
        [(2, half_reps), (2, other_reps), (1, other_reps[1::2])],
        [(3, half_reps)],
        [(3, other_reps)],
    ]
    order = jnp.stack([
        block_place[at] * 8 + r for group in sequence for at, reps in group for r in reps
    ]).astype(jnp.int32)
    parts = [rows * sum(len(reps) for _, reps in group) for group in sequence]

    link = deltas.dtype
    half_rows = rows // 2
    own_delta = deltas[0].reshape(4, 2, 2, half_rows, cols)
    weights = [
        row_weights(inner_steps, bucket_of_row, r).reshape(4, 2, 2, half_rows) for r in (rep, sibling)
    ]

    def pick(array, *index):
        starts = index + (0,) * (array.ndim - len(index))
        sizes = (1,) * len(index) + array.shape[len(index):]
        return lax.dynamic_slice(array, starts, sizes).reshape(array.shape[len(index):])

    def chip_sum(replica, part, received):
        at = replica // 2
        return (
            pick(weights[0], at, core, part)[:, None]
            * pick(own_delta, at, core, part).astype(jnp.float32)
            + pick(weights[1], at, core, part)[:, None] * pick(received, at).astype(jnp.float32)
        )

    received = []
    not_mine = 1 - core
    for part in range(2):
        theirs = lax.dynamic_slice(own_delta, (0, not_mine, part, 0, 0), (4, 1, 1, half_rows, cols))
        theirs = theirs.reshape(4, half_rows, cols)
        received.append(swap_cores(theirs))
        not_mine, theirs = together(not_mine, theirs)
    away = rep ^ first_bit
    from_first = []
    for part in range(2):
        to_first = jnp.concatenate(
            [chip_sum(block, part, received[part]) for block in (away, away ^ second_bit)], 0
        ).astype(link)
        from_first.append(swap_first(to_first))
        received, order, to_first = together(received, order, to_first)
    normed = normalize_in_order(tokens, norm_gain, order, rows, parts, 0, 2)
    own_sum = [chip_sum(rep, part, received[part]) for part in range(2)]
    next_sum = [chip_sum(rep ^ second_bit, part, received[part]) for part in range(2)]
    from_first[0], own_sum, next_sum, normed[-1] = together(from_first[0], own_sum, next_sum, normed[-1])
    from_second = []
    for part in range(2):
        next_sum[part] += from_first[part][half_rows:].astype(jnp.float32)
        own_sum[part] += from_first[part][:half_rows].astype(jnp.float32)
        to_second = next_sum[part].astype(link)
        from_second.append(swap_second(to_second))
        order, to_second = together(order, to_second)
    normed = normalize_in_order(tokens, norm_gain, order, rows, parts, 2, 2, normed)
    from_second[0], normed[-1] = together(from_second[0], normed[-1])
    from_second, own_sum = together(from_second, own_sum)
    averaged = jnp.concatenate(
        [own_sum[part] + from_second[part].astype(jnp.float32) for part in range(2)], 0
    )
    master_new, momentum_new = outer_step(averaged, master, momentum)
    layer = master_new.astype(link)

    outer = (place == 0) | (place == 3)
    pair, near_in = to_pair(layer), inwards(layer)
    pair, near_in = together(pair, near_in)
    beside = swap_first(layer)
    half0 = jnp.concatenate([layer, beside], 0)
    other0 = swap_second(half0)
    half0 = [half0, swap_cores(half0)]
    far_in, near_out = inwards(pair), outwards(near_in)
    beside = swap_first(pair)
    third1 = swap_second(pair)

    order, pair = together(order, pair)
    normed = normalize_in_order(tokens, norm_gain, order, rows, parts, 4, 4, normed)
    beside, near_out, normed[-1] = together(beside, near_out, normed[-1])
    near = jnp.where(outer, near_out, near_in)
    half1 = jnp.concatenate([pair, beside], 0)
    beside = swap_first(near)
    far_out = outwards(far_in)
    half1, half0 = together(half1, half0)
    total = project(normed[0], half0, normed[-1])
    ready = [other0, swap_cores(other0), half1, swap_cores(half1), third1, swap_cores(third1)]

    beside, total = together(beside, total)
    half2 = jnp.concatenate([near, beside], 0)
    other2 = swap_second(half2)
    far = jnp.where(outer, far_out, far_in)
    far, pair_source = together(far, other0)
    beside = swap_first(far)
    fourth1 = to_pair(pair_source[rows:])
    half2, ready = together(half2, ready)
    total = project(normed[1], ready, total)

    beside, other2, total = together(beside, other2, total)
    half3 = jnp.concatenate([far, beside], 0)
    other3 = swap_second(half3)
    ready = [half2, swap_cores(half2), other2, swap_cores(other2), fourth1, swap_cores(fourth1)]
    half3, ready = together(half3, ready)
    total = project(normed[2], ready, total)
    half3 = [half3, swap_cores(half3)]
    other3, total = together(other3, total)
    total = project(normed[3], half3, total)
    last = [other3, swap_cores(other3)]
    total = project(normed[4], last, total, True)
    return total, master_new, momentum_new


def on_any(tokens, norm_gain, deltas, inner_steps, bucket_of_row, master, momentum):
    weight = row_weights(inner_steps, bucket_of_row, lax.axis_index("rep"))
    weighted = weight[:, None] * deltas[0].astype(jnp.float32)
    averaged = lax.psum_scatter(weighted, "rep", scatter_dimension=0, tiled=True)
    master_new, momentum_new = outer_step(averaged, master, momentum)
    layer = lax.all_gather(master_new.astype(deltas.dtype), ("fsdp", "rep"), axis=0, tiled=True)
    features = tokens.shape[1]
    order = jnp.arange(features // 256, dtype=jnp.int32)
    normed, _ = normalize_in_order(tokens, norm_gain, order, 256, [features])
    keys = jnp.dot(normed, layer, preferred_element_type=jnp.float32).astype(tokens.dtype)
    return keys, master_new, momentum_new


def solution(mesh):
    in_specs = (
        P(("rep", "fsdp"), None),
        P(),
        P("rep", "fsdp", None),
        P(),
        P("fsdp"),
        P(("fsdp", "rep"), None),
        P(("fsdp", "rep"), None),
    )
    out_specs = (P(("rep", "fsdp"), None), P(("fsdp", "rep"), None), P(("fsdp", "rep"), None))
    is_block = mesh.shape["rep"] == 8 and mesh.shape["fsdp"] == 4
    return jax.shard_map(
        on_block if is_block else on_any,
        mesh=mesh, in_specs=in_specs, out_specs=out_specs, check_vma=False,
    )
```

```python
import functools

import jax
import jax.numpy as jnp
from jax import lax
from jax.experimental import pallas as pl
from jax.experimental.pallas import tpu as pltpu
from jax.sharding import PartitionSpec as P

OUTER_RATE = 0.7
MOMENTUM_KEEP = 0.9
EPSILON = 1e-05
VMEM_BYTES = 24 * 1024 * 1024

CORE, ALONG_X, ALONG_Y = 1, 2, 4


def flip(value, even_bit, odd_bit):
    perm = [(i, i ^ (odd_bit if i & CORE else even_bit)) for i in range(8)]
    return lax.ppermute(value, "rep", perm)


def swap_cores(value):
    return flip(value, CORE, CORE)


def swap_first(value):
    return flip(value, ALONG_X, ALONG_Y)


def swap_second(value):
    return flip(value, ALONG_Y, ALONG_X)


def row_weights(inner_steps, bucket_of_row, replica):
    counts = inner_steps.astype(jnp.float32)
    share = counts / jnp.sum(counts, axis=0, keepdims=True)
    own = lax.dynamic_index_in_dim(share, replica, 0, keepdims=False)
    bucket_ids = jnp.arange(counts.shape[1], dtype=jnp.int32)
    one_hot = (bucket_of_row[:, None] == bucket_ids[None, :]).astype(jnp.float32)
    return jnp.sum(one_hot * own[None, :], axis=1)


def outer_step(averaged, master, momentum):
    momentum_new = MOMENTUM_KEEP * momentum + averaged
    master_new = master - OUTER_RATE * (averaged + MOMENTUM_KEEP * momentum_new)
    return master_new, momentum_new


def normalize_kernel(order, tokens, gain, *refs, width, parts):
    outs = refs[len(refs) - parts - 1:-1]
    refs[-1][...] = jnp.zeros_like(refs[-1])
    values = tokens[...].astype(jnp.float32)
    scale = lax.rsqrt(jnp.mean(values * values, axis=1, keepdims=True) + EPSILON)
    at = 0
    for out in outs:
        for j in range(out.shape[1] // width):
            source = pl.ds(pl.multiple_of(order[at] * width, width), width)
            at += 1
            part = tokens[:, source].astype(jnp.float32) * scale * gain[:, source].astype(jnp.float32)
            out[:, j * width:(j + 1) * width] = part.astype(out.dtype)


def normalize_in_order(tokens, gain, order, width, parts, first=0, count=None, earlier=()):
    rows, features = tokens.shape
    tile = 128
    count = rows // tile if count is None else count
    return list(pl.pallas_call(
        functools.partial(normalize_kernel, width=width, parts=len(parts)),
        grid_spec=pltpu.PrefetchScalarGridSpec(
            num_scalar_prefetch=1,
            grid=(count,),
            in_specs=[
                pl.BlockSpec((tile, features), lambda i, order: (i + first, 0)),
                pl.BlockSpec((1, features), lambda i, order: (0, 0)),
            ] + [pl.BlockSpec(memory_space=pl.ANY)] * len(earlier),
            out_specs=[pl.BlockSpec((tile, part), lambda i, order: (i + first, 0)) for part in parts]
            + [pl.BlockSpec((8, 128), lambda i, order: (0, 0))],
        ),
        out_shape=[pltpu.HBM((rows, part), tokens.dtype) for part in parts]
        + [jax.ShapeDtypeStruct((8, 128), jnp.float32)],
        input_output_aliases={3 + i: i for i in range(len(earlier))},
        compiler_params=pltpu.CompilerParams(vmem_limit_bytes=VMEM_BYTES),
        cost_estimate=pl.CostEstimate(
            flops=count * tile * features * 6,
            bytes_accessed=count * tile * features * 4,
            transcendentals=count * tile,
        ),
        name="normalize_in_order",
    )(order, tokens, gain.reshape(1, features), *earlier))


def project_kernel(depths, normed, *refs):
    total = None
    start = 0
    for depth, piece in zip(depths, refs):
        term = jnp.dot(
            normed[:, start:start + depth], piece[...], preferred_element_type=jnp.float32
        )
        total = term if total is None else total + term
        start += depth
    if refs[-2].shape == total.shape:
        total = total + refs[-2][...]
    refs[-1][...] = total.astype(refs[-1].dtype)


def project(normed, pieces, total, last=False):
    rows = normed.shape[0]
    cols = pieces[0].shape[1]
    depths = [piece.shape[0] for piece in pieces]
    depth = sum(depths)
    tile = 512
    first = total.shape != (rows, cols)
    row_spec = pl.BlockSpec((tile, cols), lambda i: (i, 0))
    return pl.pallas_call(
        functools.partial(project_kernel, depths),
        grid=(rows // tile,),
        in_specs=[pl.BlockSpec((tile, depth), lambda i: (i, 0))]
        + [pl.BlockSpec(memory_space=pltpu.VMEM) for piece in pieces]
        + [pl.BlockSpec(memory_space=pl.ANY) if first else row_spec],
        out_specs=row_spec,
        out_shape=jax.ShapeDtypeStruct((rows, cols), normed.dtype if last else jnp.float32),
        compiler_params=pltpu.CompilerParams(vmem_limit_bytes=VMEM_BYTES),
        cost_estimate=pl.CostEstimate(
            flops=2 * rows * depth * cols,
            bytes_accessed=2 * (rows * depth + depth * cols) + 8 * rows * cols,
            transcendentals=0,
        ),
        name="project",
    )(normed, *pieces, total)


def together(*values):
    return lax.optimization_barrier(values)


def to_pair(value):
    return lax.ppermute(value, "fsdp", [(0, 1), (1, 0), (2, 3), (3, 2)])


def inwards(value):
    return lax.ppermute(value, "fsdp", [(1, 2), (2, 1)])


def outwards(value):
    return lax.ppermute(value, "fsdp", [(1, 0), (2, 3)])


def on_block(tokens, norm_gain, deltas, inner_steps, bucket_of_row, master, momentum):
    rep, place = lax.axis_index("rep"), lax.axis_index("fsdp")
    core = rep & 1
    sibling = rep ^ CORE
    first_bit = jnp.where(core == 0, ALONG_X, ALONG_Y)
    second_bit = jnp.where(core == 0, ALONG_Y, ALONG_X)
    rows, cols = master.shape
    tokens = pltpu.with_memory_space_constraint(tokens, pltpu.HBM)
    low = place < 2
    block_place = [place, place ^ 1, jnp.where(low, 2, 1), jnp.where(low, 3, 0)]
    half_reps = [rep, rep ^ first_bit, sibling, sibling ^ second_bit]
    other_reps = [rep ^ second_bit, rep ^ 6, sibling ^ first_bit, sibling ^ 6]
    sequence = [
        [(0, half_reps)],
        [(0, other_reps), (1, half_reps), (1, other_reps[0::2])],
        [(2, half_reps), (2, other_reps), (1, other_reps[1::2])],
        [(3, half_reps)],
        [(3, other_reps)],
    ]
    order = jnp.stack([
        block_place[at] * 8 + r for group in sequence for at, reps in group for r in reps
    ]).astype(jnp.int32)
    parts = [rows * sum(len(reps) for _, reps in group) for group in sequence]

    link = deltas.dtype
    half_rows = rows // 2
    own_delta = deltas[0].reshape(4, 2, 2, half_rows, cols)
    weights = [
        row_weights(inner_steps, bucket_of_row, r).reshape(4, 2, 2, half_rows) for r in (rep, sibling)
    ]

    def pick(array, *index):
        starts = index + (0,) * (array.ndim - len(index))
        sizes = (1,) * len(index) + array.shape[len(index):]
        return lax.dynamic_slice(array, starts, sizes).reshape(array.shape[len(index):])

    def chip_sum(replica, part, received):
        at = replica // 2
        return (
            pick(weights[0], at, core, part)[:, None]
            * pick(own_delta, at, core, part).astype(jnp.float32)
            + pick(weights[1], at, core, part)[:, None] * pick(received, at).astype(jnp.float32)
        )

    received = []
    not_mine = 1 - core
    for part in range(2):
        theirs = lax.dynamic_slice(own_delta, (0, not_mine, part, 0, 0), (4, 1, 1, half_rows, cols))
        theirs = theirs.reshape(4, half_rows, cols)
        received.append(swap_cores(theirs))
        not_mine, theirs = together(not_mine, theirs)
    away = rep ^ first_bit
    from_first = []
    for part in range(2):
        to_first = jnp.concatenate(
            [chip_sum(block, part, received[part]) for block in (away, away ^ second_bit)], 0
        ).astype(link)
        from_first.append(swap_first(to_first))
        received, order, to_first = together(received, order, to_first)
    normed = normalize_in_order(tokens, norm_gain, order, rows, parts, 0, 2)
    own_sum = [chip_sum(rep, part, received[part]) for part in range(2)]
    next_sum = [chip_sum(rep ^ second_bit, part, received[part]) for part in range(2)]
    from_first[0], own_sum, next_sum, normed[-1] = together(from_first[0], own_sum, next_sum, normed[-1])
    from_second = []
    for part in range(2):
        next_sum[part] += from_first[part][half_rows:].astype(jnp.float32)
        own_sum[part] += from_first[part][:half_rows].astype(jnp.float32)
        to_second = next_sum[part].astype(link)
        from_second.append(swap_second(to_second))
        order, to_second = together(order, to_second)
    normed = normalize_in_order(tokens, norm_gain, order, rows, parts, 2, 2, normed)
    from_second[0], normed[-1] = together(from_second[0], normed[-1])
    from_second, own_sum = together(from_second, own_sum)
    averaged = jnp.concatenate(
        [own_sum[part] + from_second[part].astype(jnp.float32) for part in range(2)], 0
    )
    master_new, momentum_new = outer_step(averaged, master, momentum)
    layer = master_new.astype(link)

    outer = (place == 0) | (place == 3)
    pair, near_in = to_pair(layer), inwards(layer)
    pair, near_in = together(pair, near_in)
    beside = swap_first(layer)
    half0 = jnp.concatenate([layer, beside], 0)
    other0 = swap_second(half0)
    half0 = [half0, swap_cores(half0)]
    far_in, near_out = inwards(pair), outwards(near_in)
    beside = swap_first(pair)
    third1 = swap_second(pair)

    order, pair = together(order, pair)
    normed = normalize_in_order(tokens, norm_gain, order, rows, parts, 4, 4, normed)
    beside, near_out, normed[-1] = together(beside, near_out, normed[-1])
    near = jnp.where(outer, near_out, near_in)
    half1 = jnp.concatenate([pair, beside], 0)
    beside = swap_first(near)
    far_out = outwards(far_in)
    half1, half0 = together(half1, half0)
    total = project(normed[0], half0, normed[-1])
    ready = [other0, swap_cores(other0), half1, swap_cores(half1), third1, swap_cores(third1)]

    beside, total = together(beside, total)
    half2 = jnp.concatenate([near, beside], 0)
    other2 = swap_second(half2)
    far = jnp.where(outer, far_out, far_in)
    far, pair_source = together(far, other0)
    beside = swap_first(far)
    fourth1 = to_pair(pair_source[rows:])
    half2, ready = together(half2, ready)
    total = project(normed[1], ready, total)

    beside, other2, total = together(beside, other2, total)
    half3 = jnp.concatenate([far, beside], 0)
    other3 = swap_second(half3)
    ready = [half2, swap_cores(half2), other2, swap_cores(other2), fourth1, swap_cores(fourth1)]
    half3, ready = together(half3, ready)
    total = project(normed[2], ready, total)
    half3 = [half3, swap_cores(half3)]
    other3, total = together(other3, total)
    total = project(normed[3], half3, total)
    last = [other3, swap_cores(other3)]
    total = project(normed[4], last, total, True)
    return total, master_new, momentum_new


def on_any(tokens, norm_gain, deltas, inner_steps, bucket_of_row, master, momentum):
    weight = row_weights(inner_steps, bucket_of_row, lax.axis_index("rep"))
    weighted = weight[:, None] * deltas[0].astype(jnp.float32)
    averaged = lax.psum_scatter(weighted, "rep", scatter_dimension=0, tiled=True)
    master_new, momentum_new = outer_step(averaged, master, momentum)
    layer = lax.all_gather(master_new.astype(deltas.dtype), ("fsdp", "rep"), axis=0, tiled=True)
    features = tokens.shape[1]
    order = jnp.arange(features // 256, dtype=jnp.int32)
    normed, _ = normalize_in_order(tokens, norm_gain, order, 256, [features])
    keys = jnp.dot(normed, layer, preferred_element_type=jnp.float32).astype(tokens.dtype)
    return keys, master_new, momentum_new


def solution(mesh):
    in_specs = (
        P(("rep", "fsdp"), None),
        P(),
        P("rep", "fsdp", None),
        P(),
        P("fsdp"),
        P(("fsdp", "rep"), None),
        P(("fsdp", "rep"), None),
    )
    out_specs = (P(("rep", "fsdp"), None), P(("fsdp", "rep"), None), P(("fsdp", "rep"), None))
    is_block = mesh.shape["rep"] == 8 and mesh.shape["fsdp"] == 4
    return jax.shard_map(
        on_block if is_block else on_any,
        mesh=mesh, in_specs=in_specs, out_specs=out_specs, check_vma=False,
    )
```

```python
import functools

import jax
import jax.numpy as jnp
from jax import lax
from jax.experimental import pallas as pl
from jax.experimental.pallas import tpu as pltpu
from jax.sharding import PartitionSpec as P

OUTER_RATE = 0.7
MOMENTUM_KEEP = 0.9
EPSILON = 1e-05
VMEM_BYTES = 24 * 1024 * 1024

CORE, ALONG_X, ALONG_Y = 1, 2, 4


def flip(value, even_bit, odd_bit):
    perm = [(i, i ^ (odd_bit if i & CORE else even_bit)) for i in range(8)]
    return lax.ppermute(value, "rep", perm)


def swap_cores(value):
    return flip(value, CORE, CORE)


def swap_first(value):
    return flip(value, ALONG_X, ALONG_Y)


def swap_second(value):
    return flip(value, ALONG_Y, ALONG_X)


def row_weights(inner_steps, bucket_of_row, replica):
    counts = inner_steps.astype(jnp.float32)
    share = counts / jnp.sum(counts, axis=0, keepdims=True)
    own = lax.dynamic_index_in_dim(share, replica, 0, keepdims=False)
    bucket_ids = jnp.arange(counts.shape[1], dtype=jnp.int32)
    one_hot = (bucket_of_row[:, None] == bucket_ids[None, :]).astype(jnp.float32)
    return jnp.sum(one_hot * own[None, :], axis=1)


def outer_step(averaged, master, momentum):
    momentum_new = MOMENTUM_KEEP * momentum + averaged
    master_new = master - OUTER_RATE * (averaged + MOMENTUM_KEEP * momentum_new)
    return master_new, momentum_new


def normalize_kernel(order, tokens, gain, *refs, width, parts):
    outs = refs[len(refs) - parts - 1:-1]
    refs[-1][...] = jnp.zeros_like(refs[-1])
    values = tokens[...].astype(jnp.float32)
    scale = lax.rsqrt(jnp.mean(values * values, axis=1, keepdims=True) + EPSILON)
    at = 0
    for out in outs:
        for j in range(out.shape[1] // width):
            source = pl.ds(pl.multiple_of(order[at] * width, width), width)
            at += 1
            part = tokens[:, source].astype(jnp.float32) * scale * gain[:, source].astype(jnp.float32)
            out[:, j * width:(j + 1) * width] = part.astype(out.dtype)


def normalize_in_order(tokens, gain, order, width, parts, first=0, count=None, earlier=()):
    rows, features = tokens.shape
    tile = 128
    count = rows // tile if count is None else count
    return list(pl.pallas_call(
        functools.partial(normalize_kernel, width=width, parts=len(parts)),
        grid_spec=pltpu.PrefetchScalarGridSpec(
            num_scalar_prefetch=1,
            grid=(count,),
            in_specs=[
                pl.BlockSpec((tile, features), lambda i, order: (i + first, 0)),
                pl.BlockSpec((1, features), lambda i, order: (0, 0)),
            ] + [pl.BlockSpec(memory_space=pl.ANY)] * len(earlier),
            out_specs=[pl.BlockSpec((tile, part), lambda i, order: (i + first, 0)) for part in parts]
            + [pl.BlockSpec((8, 128), lambda i, order: (0, 0))],
        ),
        out_shape=[pltpu.HBM((rows, part), tokens.dtype) for part in parts]
        + [jax.ShapeDtypeStruct((8, 128), jnp.float32)],
        input_output_aliases={3 + i: i for i in range(len(earlier))},
        compiler_params=pltpu.CompilerParams(vmem_limit_bytes=VMEM_BYTES),
        cost_estimate=pl.CostEstimate(
            flops=count * tile * features * 6,
            bytes_accessed=count * tile * features * 4,
            transcendentals=count * tile,
        ),
        name="normalize_in_order",
    )(order, tokens, gain.reshape(1, features), *earlier))


def project_kernel(depths, normed, *refs):
    total = None
    start = 0
    for depth, piece in zip(depths, refs):
        term = jnp.dot(
            normed[:, start:start + depth], piece[...], preferred_element_type=jnp.float32
        )
        total = term if total is None else total + term
        start += depth
    if refs[-2].shape == total.shape:
        total = total + refs[-2][...]
    refs[-1][...] = total.astype(refs[-1].dtype)


def project(normed, pieces, total, last=False):
    rows = normed.shape[0]
    cols = pieces[0].shape[1]
    depths = [piece.shape[0] for piece in pieces]
    depth = sum(depths)
    tile = 512
    first = total.shape != (rows, cols)
    row_spec = pl.BlockSpec((tile, cols), lambda i: (i, 0))
    return pl.pallas_call(
        functools.partial(project_kernel, depths),
        grid=(rows // tile,),
        in_specs=[pl.BlockSpec((tile, depth), lambda i: (i, 0))]
        + [pl.BlockSpec(memory_space=pltpu.VMEM) for piece in pieces]
        + [pl.BlockSpec(memory_space=pl.ANY) if first else row_spec],
        out_specs=row_spec,
        out_shape=jax.ShapeDtypeStruct((rows, cols), normed.dtype if last else jnp.float32),
        compiler_params=pltpu.CompilerParams(vmem_limit_bytes=VMEM_BYTES),
        cost_estimate=pl.CostEstimate(
            flops=2 * rows * depth * cols,
            bytes_accessed=2 * (rows * depth + depth * cols) + 8 * rows * cols,
            transcendentals=0,
        ),
        name="project",
    )(normed, *pieces, total)


def together(*values):
    return lax.optimization_barrier(values)


def to_pair(value):
    return lax.ppermute(value, "fsdp", [(0, 1), (1, 0), (2, 3), (3, 2)])


def inwards(value):
    return lax.ppermute(value, "fsdp", [(1, 2), (2, 1)])


def outwards(value):
    return lax.ppermute(value, "fsdp", [(1, 0), (2, 3)])


def on_block(tokens, norm_gain, deltas, inner_steps, bucket_of_row, master, momentum):
    rep, place = lax.axis_index("rep"), lax.axis_index("fsdp")
    core = rep & 1
    sibling = rep ^ CORE
    first_bit = jnp.where(core == 0, ALONG_X, ALONG_Y)
    second_bit = jnp.where(core == 0, ALONG_Y, ALONG_X)
    rows, cols = master.shape
    tokens = pltpu.with_memory_space_constraint(tokens, pltpu.HBM)
    low = place < 2
    block_place = [place, place ^ 1, jnp.where(low, 2, 1), jnp.where(low, 3, 0)]
    half_reps = [rep, rep ^ first_bit, sibling, sibling ^ second_bit]
    other_reps = [rep ^ second_bit, rep ^ 6, sibling ^ first_bit, sibling ^ 6]
    sequence = [
        [(0, half_reps)],
        [(0, other_reps), (1, half_reps), (1, other_reps[0::2])],
        [(2, half_reps), (2, other_reps), (1, other_reps[1::2])],
        [(3, half_reps)],
        [(3, other_reps)],
    ]
    order = jnp.stack([
        block_place[at] * 8 + r for group in sequence for at, reps in group for r in reps
    ]).astype(jnp.int32)
    parts = [rows * sum(len(reps) for _, reps in group) for group in sequence]

    link = deltas.dtype
    half_rows = rows // 2
    own_delta = deltas[0].reshape(4, 2, 2, half_rows, cols)
    weights = [
        row_weights(inner_steps, bucket_of_row, r).reshape(4, 2, 2, half_rows) for r in (rep, sibling)
    ]

    def pick(array, *index):
        starts = index + (0,) * (array.ndim - len(index))
        sizes = (1,) * len(index) + array.shape[len(index):]
        return lax.dynamic_slice(array, starts, sizes).reshape(array.shape[len(index):])

    def chip_sum(replica, part, received):
        at = replica // 2
        return (
            pick(weights[0], at, core, part)[:, None]
            * pick(own_delta, at, core, part).astype(jnp.float32)
            + pick(weights[1], at, core, part)[:, None] * pick(received, at).astype(jnp.float32)
        )

    received = []
    not_mine = 1 - core
    for part in range(2):
        theirs = lax.dynamic_slice(own_delta, (0, not_mine, part, 0, 0), (4, 1, 1, half_rows, cols))
        theirs = theirs.reshape(4, half_rows, cols)
        received.append(swap_cores(theirs))
        not_mine, theirs = together(not_mine, theirs)
    away = rep ^ first_bit
    from_first = []
    for part in range(2):
        to_first = jnp.concatenate(
            [chip_sum(block, part, received[part]) for block in (away, away ^ second_bit)], 0
        ).astype(link)
        from_first.append(swap_first(to_first))
        received, order, to_first = together(received, order, to_first)
    normed = normalize_in_order(tokens, norm_gain, order, rows, parts, 0, 2)
    own_sum = [chip_sum(rep, part, received[part]) for part in range(2)]
    next_sum = [chip_sum(rep ^ second_bit, part, received[part]) for part in range(2)]
    from_first[0], own_sum, next_sum, normed[-1] = together(from_first[0], own_sum, next_sum, normed[-1])
    from_second = []
    for part in range(2):
        next_sum[part] += from_first[part][half_rows:].astype(jnp.float32)
        own_sum[part] += from_first[part][:half_rows].astype(jnp.float32)
        to_second = next_sum[part].astype(link)
        from_second.append(swap_second(to_second))
        order, to_second = together(order, to_second)
    normed = normalize_in_order(tokens, norm_gain, order, rows, parts, 2, 2, normed)
    from_second[0], normed[-1] = together(from_second[0], normed[-1])
    from_second, own_sum = together(from_second, own_sum)
    averaged = jnp.concatenate(
        [own_sum[part] + from_second[part].astype(jnp.float32) for part in range(2)], 0
    )
    master_new, momentum_new = outer_step(averaged, master, momentum)
    layer = master_new.astype(link)

    outer = (place == 0) | (place == 3)
    pair, near_in = to_pair(layer), inwards(layer)
    pair, near_in = together(pair, near_in)
    beside = swap_first(layer)
    half0 = jnp.concatenate([layer, beside], 0)
    other0 = swap_second(half0)
    half0 = [half0, swap_cores(half0)]
    far_in, near_out = inwards(pair), outwards(near_in)
    beside = swap_first(pair)
    third1 = swap_second(pair)

    order, pair = together(order, pair)
    normed = normalize_in_order(tokens, norm_gain, order, rows, parts, 4, 4, normed)
    near_out, normed[-1] = together(near_out, normed[-1])
    near = jnp.where(outer, near_out, near_in)
    half1 = jnp.concatenate([pair, beside], 0)
    beside = swap_first(near)
    far_out = outwards(far_in)
    half1, half0 = together(half1, half0)
    total = project(normed[0], half0, normed[-1])
    ready = [other0, swap_cores(other0), half1, swap_cores(half1), third1, swap_cores(third1)]

    beside, total = together(beside, total)
    half2 = jnp.concatenate([near, beside], 0)
    other2 = swap_second(half2)
    far = jnp.where(outer, far_out, far_in)
    far, pair_source = together(far, other0)
    beside = swap_first(far)
    fourth1 = to_pair(pair_source[rows:])
    half2, ready = together(half2, ready)
    total = project(normed[1], ready, total)

    beside, other2, total = together(beside, other2, total)
    half3 = jnp.concatenate([far, beside], 0)
    other3 = swap_second(half3)
    ready = [half2, swap_cores(half2), other2, swap_cores(other2), fourth1, swap_cores(fourth1)]
    half3, ready = together(half3, ready)
    total = project(normed[2], ready, total)
    half3 = [half3, swap_cores(half3)]
    other3, total = together(other3, total)
    total = project(normed[3], half3, total)
    last = [other3, swap_cores(other3)]
    total = project(normed[4], last, total, True)
    return total, master_new, momentum_new


def on_any(tokens, norm_gain, deltas, inner_steps, bucket_of_row, master, momentum):
    weight = row_weights(inner_steps, bucket_of_row, lax.axis_index("rep"))
    weighted = weight[:, None] * deltas[0].astype(jnp.float32)
    averaged = lax.psum_scatter(weighted, "rep", scatter_dimension=0, tiled=True)
    master_new, momentum_new = outer_step(averaged, master, momentum)
    layer = lax.all_gather(master_new.astype(deltas.dtype), ("fsdp", "rep"), axis=0, tiled=True)
    features = tokens.shape[1]
    order = jnp.arange(features // 256, dtype=jnp.int32)
    normed, _ = normalize_in_order(tokens, norm_gain, order, 256, [features])
    keys = jnp.dot(normed, layer, preferred_element_type=jnp.float32).astype(tokens.dtype)
    return keys, master_new, momentum_new


def solution(mesh):
    in_specs = (
        P(("rep", "fsdp"), None),
        P(),
        P("rep", "fsdp", None),
        P(),
        P("fsdp"),
        P(("fsdp", "rep"), None),
        P(("fsdp", "rep"), None),
    )
    out_specs = (P(("rep", "fsdp"), None), P(("fsdp", "rep"), None), P(("fsdp", "rep"), None))
    is_block = mesh.shape["rep"] == 8 and mesh.shape["fsdp"] == 4
    return jax.shard_map(
        on_block if is_block else on_any,
        mesh=mesh, in_specs=in_specs, out_specs=out_specs, check_vma=False,
    )
```
